32 devices in a mesh: pair: 2 (over x), grp: 2 (over core), proc: 8 (over z, y).
Axes of the slice: x: 2, y: 2, z: 4, core: 2. Of those that a mesh axis runs over, the one named last changes fastest.
Arguments:
- child_factor: bfloat16 [2, 24, 8, 128, 4096], P('pair', 'grp', 'proc'), parts along dimension 1, may hold values from -0.044194174 to 0.044194174
- child_update: float32 [2, 24, 8, 128, 1024], P('pair', 'grp', 'proc'), parts along dimension 1, may hold values from -0.2 to 0.2
- child_map: int32 [2, 192], P(None, 'grp'), parts along dimension 1, may hold values from 0 to 191, as said below
- parent_entries: float32 [48, 8, 128, 4, 2, 128], P('grp', 'proc', None, None, 'pair'), parts along dimension 0, may hold values from -0.3 to 10.3, as said below
Outputs:
- parent_factor: float32 [48, 8, 128, 4, 2, 128], P('grp', 'proc', None, None, 'pair'), parts along dimension 0
The draws below stay inside these ranges and needn't reach their ends.
There are 2 independent parts, one for each index of `grp`. The reference program is written for one: setup_inputs(seed, part) draws one part's arguments, and reference() takes and returns one part's arrays. A program takes and returns all parts, laid end to end along the dimension named above; each array names one. Nothing has to cross between parts.
Inputs may be any that keep to these rules, and one draw needn't show every extreme that they name: `child_map`: for each child the map is one to one; the child row blocks held at [c, r, s] for one r go to parent row blocks q * 8 + d with one q and every d once; each child maps exactly 8 row blocks onto parent blocks 0 to 7; one device of a child sends at most 2 row blocks to parent blocks with one value of d, and reaches 2. `parent_entries`: off the diagonal entries are small; the diagonal is positive and dominant.
All inputs are finite; a program needn't handle non-finite values.
Results may differ from the reference program's by a relative error of at most 0.00095.
Values may be sent and summed in bfloat16 or wider, within the bound.
A program may use at most 128 MiB of HBM per device.

```python
import jax
import jax.numpy as jnp
from jax import lax

CU = 12288
KC = 4096
PANELS = 2
WB = 8
PB = 192
CUB = 96
WIN = 1024
N_PAIR = 2
N_PROC = 8


def child_order(key, child):
    key = jax.random.fold_in(key, child)
    local_count = CUB // N_PROC
    local_total = PB // N_PROC
    window_seats = -(-WB // N_PROC)
    rotation = jax.random.permutation(jax.random.fold_in(key, 1), local_count)
    others = jax.random.permutation(jax.random.fold_in(key, 2), local_total - window_seats) + window_seats
    chosen = jnp.concatenate([jnp.arange(window_seats), others])[:local_count]
    chosen = chosen[jax.random.permutation(jax.random.fold_in(key, 3), local_count)]
    proc_of = (jnp.arange(N_PROC)[None, :] + rotation[:, None]) % N_PROC
    return (chosen[:, None] * N_PROC + proc_of).reshape(CUB).astype(jnp.int32)


def draw_child_map(key, part):
    key = jax.random.fold_in(key, 11)
    key = jax.random.fold_in(key, part)
    return jnp.stack([child_order(key, 0), child_order(key, 1)])


def draw_child_factor(key, part):
    key = jax.random.fold_in(key, 31)
    key = jax.random.fold_in(key, part)
    shape = (N_PAIR, CUB // N_PROC, N_PROC, 128, KC)
    spread = (2.0 * KC) ** (-0.5)
    values = jnp.clip(spread * jax.random.normal(key, shape, jnp.float32), -4.0 * spread, 4.0 * spread)
    return values.astype(jnp.bfloat16)


def draw_child_update(key, part):
    key = jax.random.fold_in(key, 37)
    key = jax.random.fold_in(key, part)
    shape = (N_PAIR, CUB // N_PROC, N_PROC, 128, WIN)
    values = jnp.clip(0.05 * jax.random.normal(key, shape, jnp.float32), -0.2, 0.2)
    return values.astype(jnp.float32)


def draw_parent_entries(key, part):
    key = jax.random.fold_in(key, 23)
    key = jax.random.fold_in(key, part)
    shape = (PB // N_PROC, N_PROC, 128, WB // 2, 2, 128)
    noise = jnp.clip(0.05 * jax.random.normal(jax.random.fold_in(key, 1), shape, jnp.float32), -0.3, 0.3)
    row_pos = (jnp.arange(PB // N_PROC).reshape(-1, 1, 1, 1, 1, 1) * N_PROC + jnp.arange(N_PROC).reshape(1, -1, 1, 1, 1, 1)) * 128 + jnp.arange(128).reshape(1, 1, -1, 1, 1, 1)
    col_pos = (jnp.arange(WB // 2).reshape(1, 1, 1, -1, 1, 1) * 2 + jnp.arange(2).reshape(1, 1, 1, 1, -1, 1)) * 128 + jnp.arange(128).reshape(1, 1, 1, 1, 1, -1)
    diag_value = jax.random.uniform(jax.random.fold_in(key, 2), shape, jnp.float32, 6.0, 10.0)
    return jnp.where(row_pos == col_pos, diag_value, noise).astype(jnp.float32)


def setup_inputs(seed: int = 0, part: int = 0) -> dict:
    key_list = jax.random.split(jax.random.key(seed), 5)
    own_keys = jax.random.split(jax.random.fold_in(key_list[4], part), 5)
    return {
        "child_factor": draw_child_factor(jax.random.fold_in(jax.random.fold_in(key_list[4], part), 71), part),
        "child_update": draw_child_update(jax.random.fold_in(jax.random.fold_in(key_list[4], part), 71), part),
        "child_map": draw_child_map(jax.random.fold_in(jax.random.fold_in(key_list[4], part), 71), part),
        "parent_entries": draw_parent_entries(jax.random.fold_in(jax.random.fold_in(key_list[4], part), 71), part),
    }


def sym_factor(diag_block):
    return jnp.linalg.cholesky(jnp.tril(diag_block) + jnp.tril(diag_block, -1).T)

def reference(child_factor, child_update, child_map, parent_entries):
    factor = child_factor.reshape(N_PAIR, CUB, 128, KC)
    update = child_update.reshape(N_PAIR, CUB, 128, WIN)
    matrix = parent_entries.reshape(PB, 128, WB, 128)
    for child in range(N_PAIR):
        block_map = child_map[child]
        window_at = jnp.argmax((block_map[None, :] == jnp.arange(WB)[:, None]).astype(jnp.int32), axis=1)
        window = factor[child][window_at].reshape(WIN, KC)
        product = jnp.dot(factor[child].reshape(CU, KC).astype(jnp.float32), window.T.astype(jnp.float32), preferred_element_type=jnp.float32)
        contrib = update[child].reshape(CU, WIN) - product
        matrix = matrix.at[block_map].add(contrib.reshape(CUB, 128, WB, 128))
    rows_all = jnp.arange(PB)
    cols_all = jnp.arange(WB)
    for panel_idx in range(PANELS):
        pivot_factor = sym_factor(matrix[panel_idx, :, panel_idx, :])
        column = matrix[:, :, panel_idx, :].reshape(PB * 128, 128)
        solved = lax.linalg.triangular_solve(pivot_factor, column, left_side=False, lower=True, transpose_a=True).reshape(PB, 128, 128)
        panel_rows = jnp.where((rows_all > panel_idx)[:, None, None], solved, jnp.where((rows_all == panel_idx)[:, None, None], pivot_factor[None], jnp.zeros_like(solved)))
        change = jnp.einsum('qax,hbx->qahb', panel_rows, panel_rows[:WB], precision=lax.Precision.HIGHEST)
        trailing = (cols_all > panel_idx)[None, None, :, None]
        is_panel = (cols_all == panel_idx)[None, None, :, None]
        matrix = jnp.where(is_panel, panel_rows[:, :, None, :], matrix - jnp.where(trailing, change, jnp.zeros_like(change)))
    row_idx = jnp.arange(PB * 128).reshape(PB, 128)
    col_idx = jnp.arange(WIN).reshape(WB, 128)
    lower_part = row_idx[:, :, None, None] >= col_idx[None, None, :, :]
    result = jnp.where(lower_part, matrix, jnp.zeros_like(matrix))
    return result.reshape(PB // N_PROC, N_PROC, 128, WB // 2, 2, 128)
```

```python
import functools

import jax
import jax.numpy as jnp
from jax import lax
from jax.experimental import pallas as pl
from jax.experimental.pallas import tpu as pltpu
from jax.sharding import PartitionSpec as P

HIGHEST = lax.Precision.HIGHEST
NT = (((1,), (1,)), ((), ()))
LINK = jnp.float16
VMEM_LIMIT = 60 * 1024 * 1024


def nt_dot(a, b):
    return lax.dot_general(a, b, NT, precision=HIGHEST, preferred_element_type=jnp.float32)


def contrib_kernel(half, slots, seats, factor_ref, update_ref, *rest):
    window_refs, out_ref, window = rest[: 2 * half], rest[2 * half], rest[2 * half + 1]

    @pl.when(pl.program_id(0) == 0)
    def _():
        for p in range(2):
            for h in range(half):
                window[p, h * 128 : (h + 1) * 128, :] = window_refs[2 * h + p][0]

    for p in range(2):
        product = lax.dot_general(
            factor_ref[0], window[p], NT, preferred_element_type=jnp.float32
        )
        for h in range(half):
            w = 2 * h + p
            out_ref[p, 0, :, h * 128 : (h + 1) * 128] = (
                update_ref[0, :, w * 128 : (w + 1) * 128] - product[:, h * 128 : (h + 1) * 128]
            ).astype(out_ref.dtype)


def contrib_blocks(factor, update, gathered, slots, seats, slot_count):
    rows, _, pivots = factor.shape
    cols = update.shape[2]
    half = cols // 256

    def seat_map(w):
        return lambda i, slots, seats: (seats[w], 0, 0)

    return pl.pallas_call(
        functools.partial(contrib_kernel, half),
        out_shape=jax.ShapeDtypeStruct((2, slot_count, 128, half * 128), jnp.float32),
        grid_spec=pltpu.PrefetchScalarGridSpec(
            num_scalar_prefetch=2,
            grid=(rows,),
            in_specs=[
                pl.BlockSpec((1, 128, pivots), lambda i, slots, seats: (i, 0, 0)),
                pl.BlockSpec((1, 128, cols), lambda i, slots, seats: (i, 0, 0)),
            ]
            + [pl.BlockSpec((1, 128, pivots), seat_map(w)) for w in range(2 * half)],
            out_specs=pl.BlockSpec(
                (2, 1, 128, half * 128), lambda i, slots, seats: (0, slots[i], 0, 0)
            ),
            scratch_shapes=[pltpu.VMEM((2, half * 128, pivots), jnp.bfloat16)],
        ),
        compiler_params=pltpu.CompilerParams(vmem_limit_bytes=VMEM_LIMIT),
        name="contrib",
    )(slots, seats, factor, update, *([gathered] * (2 * half)))


def column_kernel(group, half, where, entries_ref, *rest):
    arrived, out_ref = rest[: 2 * group], rest[2 * group]
    step = pl.program_id(0)
    count = where.shape[0] // 2
    for g in range(group):
        value = entries_ref[g, pl.ds(0, 128, stride=half), :]
        for c in range(2):
            spot = where[c * count + step * group + g]
            part = arrived[2 * g + c][0].astype(jnp.float32)
            value = value + jnp.where(spot >= 0, part, 0.0)
        out_ref[g] = value


def arrived_specs(group, count, width):
    def spot(c, g):
        return lambda i, where, *more: (jnp.maximum(where[c * count + i * group + g], 0), 0, 0)

    return [pl.BlockSpec((1, 128, width), spot(c, g)) for g in range(group) for c in range(2)]


def raw_column(entries, arrived, where, group):
    count, rows, _ = entries.shape
    half = rows // 128
    return pl.pallas_call(
        functools.partial(column_kernel, group, half),
        out_shape=jax.ShapeDtypeStruct((count, 128, 128), jnp.float32),
        grid_spec=pltpu.PrefetchScalarGridSpec(
            num_scalar_prefetch=1,
            grid=(count // group,),
            in_specs=[pl.BlockSpec((group, rows, 128), lambda i, where: (i, 0, 0))]
            + arrived_specs(group, count, 128),
            out_specs=pl.BlockSpec((group, 128, 128), lambda i, where: (i, 0, 0)),
        ),
        compiler_params=pltpu.CompilerParams(vmem_limit_bytes=VMEM_LIMIT),
        name="raw_column",
    )(where, entries, *([arrived] * (2 * group)))


def finish_kernel(group, half, where, place, entries_ref, zero_ref, one_ref, small_ref, lead_ref, *rest):
    arrived, out_ref = rest[: 2 * group], rest[2 * group]
    step = pl.program_id(0)
    count = where.shape[0] // 2
    my_proc, my_pair, proc_count = place[0], place[1], place[2]
    rows = group * 128
    block = (step * group + lax.broadcasted_iota(jnp.int32, (rows, 1), 0) // 128) * proc_count + my_proc

    def spread(k):
        return jnp.broadcast_to(small_ref[k][None], (group, 128, 128)).reshape(rows, 128)

    first = nt_dot(zero_ref[...].reshape(rows, 128), small_ref[0])
    first = jnp.where(block > 0, first, spread(1))
    second = nt_dot(one_ref[...].reshape(rows, 128) - nt_dot(first, small_ref[4]), small_ref[2])
    second = jnp.where(block > 1, second, jnp.where(block == 1, spread(3), 0.0))
    change = nt_dot(jnp.concatenate([first, second], axis=1), lead_ref[128:, :])
    row_id = block * 128 + lax.broadcasted_iota(jnp.int32, (rows, 1), 0) % 128
    lane = lax.broadcasted_iota(jnp.int32, (1, 128), 1)
    panel = jnp.where(my_pair == 0, first, second)
    for h in range(half):
        lower = row_id >= (2 * h + my_pair) * 128 + lane
        for g in range(group):
            span = slice(g * 128, (g + 1) * 128)
            if h == 0:
                value = panel[span]
            else:
                value = entries_ref[g, pl.ds(h, 128, stride=half), :]
                for c in range(2):
                    spot = where[c * count + step * group + g]
                    part = arrived[2 * g + c][0, :, h * 128 : (h + 1) * 128].astype(jnp.float32)
                    value = value + jnp.where(spot >= 0, part, 0.0)
                value = value - change[span, (h - 1) * 128 : h * 128]
            out_ref[g, pl.ds(h, 128, stride=half), :] = jnp.where(lower[span], value, 0.0)


def finish(entries, arrived, where, place, zero, one, small, lead, group):
    count, rows, _ = entries.shape
    half = rows // 128
    by_row = lambda i, where, place: (i, 0, 0)
    return pl.pallas_call(
        functools.partial(finish_kernel, group, half),
        out_shape=jax.ShapeDtypeStruct(entries.shape, jnp.float32),
        grid_spec=pltpu.PrefetchScalarGridSpec(
            num_scalar_prefetch=2,
            grid=(count // group,),
            in_specs=[
                pl.BlockSpec((group, rows, 128), by_row),
                pl.BlockSpec((group, 128, 128), by_row),
                pl.BlockSpec((group, 128, 128), by_row),
                pl.BlockSpec(small.shape, lambda i, where, place: (0, 0, 0)),
                pl.BlockSpec(lead.shape, lambda i, where, place: (0, 0)),
            ]
            + arrived_specs(group, count, half * 128),
            out_specs=pl.BlockSpec((group, rows, 128), by_row),
        ),
        compiler_params=pltpu.CompilerParams(vmem_limit_bytes=VMEM_LIMIT),
        name="finish",
    )(where, place, entries, zero, one, small, lead, *([arrived] * (2 * group)))


def pivot_of(block):
    pivot = jnp.linalg.cholesky(jnp.tril(block) + jnp.tril(block, -1).T)
    inverse = lax.linalg.triangular_solve(
        pivot, jnp.eye(128, dtype=jnp.float32), left_side=True, lower=True
    )
    return pivot, inverse


def times_t(a, b):
    return jnp.einsum("qax,bx->qab", a, b, precision=HIGHEST)


def body(child_factor, child_update, child_map, parent_entries):
    proc_count = lax.axis_size("proc")
    pair_count = lax.axis_size("pair")
    my_proc = lax.axis_index("proc")
    my_pair = lax.axis_index("pair")
    _, local_count, _, _, pivots = child_factor.shape
    window_cols = child_update.shape[4]
    block_cols = window_cols // 128
    half = block_cols // 2
    capacity = -(-local_count // proc_count)
    slot_count = proc_count * capacity
    local_rows = parent_entries.shape[0]
    factor = child_factor.reshape(local_count, 128, pivots)
    update = child_update.reshape(local_count, 128, window_cols)
    entries = parent_entries.reshape(local_rows, 128 * half, 128)

    all_maps = child_map.reshape(pair_count, local_count, proc_count)
    child_maps = lax.dynamic_index_in_dim(all_maps, my_pair, 0, False)
    lead_at = jnp.argmax((child_maps < proc_count).astype(jnp.int32), axis=0)
    lead_ids = jnp.min(jnp.where(child_maps < proc_count, child_maps, proc_count), axis=0)
    seats = jnp.argmax(
        (lead_ids[None, :] == jnp.arange(block_cols)[:, None]).astype(jnp.int32), axis=1
    ).astype(jnp.int32)
    own_blocks = lax.dynamic_index_in_dim(child_maps, my_proc, 1, False)
    target = own_blocks % proc_count
    order = jnp.arange(local_count)
    rank = jnp.sum(
        ((target[:, None] == target[None, :]) & (order[None, :] < order[:, None])).astype(jnp.int32),
        axis=1,
    )
    slots = (target * capacity + rank).astype(jnp.int32)
    hit = all_maps % proc_count == my_proc
    hit_rank = jnp.cumsum(hit.astype(jnp.int32), axis=1) - 1
    source = (
        jnp.arange(pair_count)[:, None, None] * proc_count + jnp.arange(proc_count)[None, None, :]
    ) * capacity + hit_rank
    match = hit[..., None] & (all_maps[..., None] // proc_count == jnp.arange(local_rows))
    where = jnp.max(jnp.where(match, source[..., None], -1), axis=(1, 2))
    where = where.reshape(pair_count * local_rows).astype(jnp.int32)

    picked = lax.dynamic_index_in_dim(
        factor, lax.dynamic_index_in_dim(lead_at, my_proc, 0, False), 0, True
    )
    gathered = lax.all_gather(picked, "proc", axis=0, tiled=True)
    packed = contrib_blocks(factor, update, gathered, slots, seats, slot_count)
    arrived = lax.all_to_all(
        packed.astype(LINK).reshape(pair_count * proc_count, capacity, 128, half * 128),
        ("pair", "proc"),
        split_axis=0,
        concat_axis=0,
        tiled=True,
    ).reshape(pair_count * slot_count, 128, half * 128)
    arrived = arrived.astype(jnp.float32)

    column = raw_column(entries, arrived, where, 4)
    lead = lax.all_gather(column[0], ("pair", "proc"), axis=0, tiled=False)
    lead = lead.reshape(2, proc_count, 128, 128)
    other = lax.ppermute(column.astype(LINK), "pair", [(0, 1), (1, 0)]).astype(jnp.float32)
    other_lead = lax.dynamic_index_in_dim(
        lax.dynamic_index_in_dim(lead, 1 - my_pair, 0, False), my_proc, 0, True
    )
    other = jnp.concatenate([other_lead, other[1:]], axis=0)
    zero = jnp.where(my_pair == 0, column, other)
    one = jnp.where(my_pair == 0, other, column)

    ids = jnp.arange(block_cols)[:, None, None]
    pivot0, inverse0 = pivot_of(lead[0, 0])
    first = jnp.where(ids > 0, times_t(lead[0, :block_cols], inverse0), pivot0)
    rest = lead[1, :block_cols] - times_t(first, first[1])
    pivot1, inverse1 = pivot_of(rest[1])
    second = jnp.where(ids > 1, times_t(rest, inverse1), jnp.where(ids == 1, pivot1, 0.0))
    both = jnp.concatenate([first, second], axis=2)
    mine = lax.dynamic_index_in_dim(both.reshape(half, 2, 128, 256), my_pair, 1, False)
    small = jnp.stack([inverse0, pivot0, inverse1, pivot1, first[1]])
    place = jnp.stack([my_proc, my_pair, jnp.int32(proc_count)]).astype(jnp.int32)
    result = finish(
        entries, arrived, where, place, zero, one, small, mine.reshape(half * 128, 256), 4
    )
    return result.reshape(local_rows, 1, 128, half, 1, 128)


def solution(mesh):
    in_specs = (
        P("pair", "grp", "proc", None, None),
        P("pair", "grp", "proc", None, None),
        P(None, "grp"),
        P("grp", "proc", None, None, "pair", None),
    )
    out_specs = P("grp", "proc", None, None, "pair", None)
    return jax.shard_map(body, mesh=mesh, in_specs=in_specs, out_specs=out_specs, check_vma=False)
```

```python
import functools

import jax
import jax.numpy as jnp
from jax import lax
from jax.experimental import pallas as pl
from jax.experimental.pallas import tpu as pltpu
from jax.sharding import PartitionSpec as P

HIGHEST = lax.Precision.HIGHEST
NT = (((1,), (1,)), ((), ()))
PANELS = 2
LINK = jnp.float16
VMEM_LIMIT = 60 * 1024 * 1024


def nt_dot(a, b):
    return lax.dot_general(a, b, NT, precision=HIGHEST, preferred_element_type=jnp.float32)


def contrib_kernel(group, half, slots, seats, factor_ref, update_ref, *rest):
    window_refs, out_ref, window = rest[: 2 * half], rest[2 * half], rest[2 * half + 1]
    step = pl.program_id(0)

    @pl.when(step == 0)
    def _():
        for p in range(2):
            for h in range(half):
                window[p, h * 128 : (h + 1) * 128, :] = window_refs[2 * h + p][0]

    pivots = factor_ref.shape[2]
    rows = factor_ref[...].reshape(group * 128, pivots)
    for p in range(2):
        product = lax.dot_general(rows, window[p], NT, preferred_element_type=jnp.float32)
        for g in range(group):
            slot = slots[step * group + g]
            for h in range(half):
                w = 2 * h + p
                out_ref[p, slot, :, h * 128 : (h + 1) * 128] = (
                    update_ref[g, :, w * 128 : (w + 1) * 128]
                    - product[g * 128 : (g + 1) * 128, h * 128 : (h + 1) * 128]
                ).astype(out_ref.dtype)


def contrib_blocks(factor, update, gathered, slots, seats, slot_count, group):
    rows, _, pivots = factor.shape
    cols = update.shape[2]
    half = cols // 256
    once = pl.Buffered(1)

    def seat_map(w):
        return lambda i, slots, seats: (seats[w], 0, 0)

    return pl.pallas_call(
        functools.partial(contrib_kernel, group, half),
        out_shape=jax.ShapeDtypeStruct((2, slot_count, 128, half * 128), jnp.float32),
        grid_spec=pltpu.PrefetchScalarGridSpec(
            num_scalar_prefetch=2,
            grid=(rows // group,),
            in_specs=[
                pl.BlockSpec((group, 128, pivots), lambda i, slots, seats: (i, 0, 0)),
                pl.BlockSpec((group, 128, cols), lambda i, slots, seats: (i, 0, 0)),
            ]
            + [
                pl.BlockSpec((1, 128, pivots), seat_map(w), pipeline_mode=once)
                for w in range(2 * half)
            ],
            out_specs=pl.BlockSpec(
                (2, slot_count, 128, half * 128),
                lambda i, slots, seats: (0, 0, 0, 0),
                pipeline_mode=once,
            ),
            scratch_shapes=[pltpu.VMEM((2, half * 128, pivots), jnp.bfloat16)],
        ),
        cost_estimate=pl.CostEstimate(
            flops=2 * rows * 128 * cols * pivots,
            bytes_accessed=rows * 128 * (2 * pivots + 6 * cols) + 2 * cols * pivots,
            transcendentals=0,
        ),
        compiler_params=pltpu.CompilerParams(vmem_limit_bytes=VMEM_LIMIT),
        name="contrib",
    )(slots, seats, factor, update, *([gathered] * (2 * half)))


def column_kernel(group, half, where, entries_ref, *rest):
    arrived, out_ref = rest[: 2 * group], rest[2 * group]
    step = pl.program_id(0)
    count = where.shape[0] // 2
    for g in range(group):
        value = entries_ref[g, pl.ds(0, 128, stride=half), :]
        for c in range(2):
            spot = where[c * count + step * group + g]
            part = arrived[2 * g + c][0].astype(jnp.float32)
            value = value + jnp.where(spot >= 0, part, 0.0)
        out_ref[g] = value


def arrived_specs(group, count, width):
    def spot(c, g):
        return lambda i, where, *more: (jnp.maximum(where[c * count + i * group + g], 0), 0, 0)

    return [pl.BlockSpec((1, 128, width), spot(c, g)) for g in range(group) for c in range(2)]


def raw_column(entries, arrived, where, group):
    count, rows, _ = entries.shape
    half = rows // 128
    return pl.pallas_call(
        functools.partial(column_kernel, group, half),
        out_shape=jax.ShapeDtypeStruct((count, 128, 128), jnp.float32),
        grid_spec=pltpu.PrefetchScalarGridSpec(
            num_scalar_prefetch=1,
            grid=(count // group,),
            in_specs=[pl.BlockSpec((group, rows, 128), lambda i, where: (i, 0, 0))]
            + arrived_specs(group, count, 128),
            out_specs=pl.BlockSpec((group, 128, 128), lambda i, where: (i, 0, 0)),
        ),
        compiler_params=pltpu.CompilerParams(vmem_limit_bytes=VMEM_LIMIT),
        name="raw_column",
    )(where, entries, *([arrived] * (2 * group)))


def finish_kernel(group, half, where, place, entries_ref, zero_ref, one_ref, small_ref, lead_ref, *rest):
    arrived, out_ref = rest[: 2 * group], rest[2 * group]
    step = pl.program_id(0)
    count = where.shape[0] // 2
    my_proc, my_pair, proc_count = place[0], place[1], place[2]
    rows = group * 128
    block = (step * group + lax.broadcasted_iota(jnp.int32, (rows, 1), 0) // 128) * proc_count + my_proc

    def spread(k):
        return jnp.broadcast_to(small_ref[k][None], (group, 128, 128)).reshape(rows, 128)

    first = nt_dot(zero_ref[...].reshape(rows, 128), small_ref[0])
    first = jnp.where(block > 0, first, spread(1))
    second = nt_dot(one_ref[...].reshape(rows, 128) - nt_dot(first, small_ref[4]), small_ref[2])
    second = jnp.where(block > 1, second, jnp.where(block == 1, spread(3), 0.0))
    change = nt_dot(jnp.concatenate([first, second], axis=1), lead_ref[128:, :])
    row_id = block * 128 + lax.broadcasted_iota(jnp.int32, (rows, 1), 0) % 128
    lane = lax.broadcasted_iota(jnp.int32, (1, 128), 1)
    panel = jnp.where(my_pair == 0, first, second)
    for h in range(half):
        lower = row_id >= (2 * h + my_pair) * 128 + lane
        for g in range(group):
            span = slice(g * 128, (g + 1) * 128)
            if h == 0:
                value = panel[span]
            else:
                value = entries_ref[g, pl.ds(h, 128, stride=half), :]
                for c in range(2):
                    spot = where[c * count + step * group + g]
                    part = arrived[2 * g + c][0, :, h * 128 : (h + 1) * 128].astype(jnp.float32)
                    value = value + jnp.where(spot >= 0, part, 0.0)
                value = value - change[span, (h - 1) * 128 : h * 128]
            out_ref[g, pl.ds(h, 128, stride=half), :] = jnp.where(lower[span], value, 0.0)


def finish(entries, arrived, where, place, zero, one, small, lead, group):
    count, rows, _ = entries.shape
    half = rows // 128
    by_row = lambda i, where, place: (i, 0, 0)
    return pl.pallas_call(
        functools.partial(finish_kernel, group, half),
        out_shape=jax.ShapeDtypeStruct(entries.shape, jnp.float32),
        grid_spec=pltpu.PrefetchScalarGridSpec(
            num_scalar_prefetch=2,
            grid=(count // group,),
            in_specs=[
                pl.BlockSpec((group, rows, 128), by_row),
                pl.BlockSpec((group, 128, 128), by_row),
                pl.BlockSpec((group, 128, 128), by_row),
                pl.BlockSpec(small.shape, lambda i, where, place: (0, 0, 0)),
                pl.BlockSpec(lead.shape, lambda i, where, place: (0, 0)),
            ]
            + arrived_specs(group, count, half * 128),
            out_specs=pl.BlockSpec((group, rows, 128), by_row),
        ),
        compiler_params=pltpu.CompilerParams(vmem_limit_bytes=VMEM_LIMIT),
        name="finish",
    )(where, place, entries, zero, one, small, lead, *([arrived] * (2 * group)))


def pivot_of(block):
    pivot = jnp.linalg.cholesky(jnp.tril(block) + jnp.tril(block, -1).T)
    inverse = lax.linalg.triangular_solve(
        pivot, jnp.eye(128, dtype=jnp.float32), left_side=True, lower=True
    )
    return pivot, inverse


def times_t(a, b):
    return jnp.einsum("qax,bx->qab", a, b, precision=HIGHEST)


def body(child_factor, child_update, child_map, parent_entries):
    proc_count = lax.axis_size("proc")
    pair_count = lax.axis_size("pair")
    my_proc = lax.axis_index("proc")
    my_pair = lax.axis_index("pair")
    _, local_count, _, _, pivots = child_factor.shape
    window_cols = child_update.shape[4]
    block_cols = window_cols // 128
    half = block_cols // 2
    capacity = -(-local_count // proc_count)
    slot_count = proc_count * capacity
    local_rows = parent_entries.shape[0]
    factor = child_factor.reshape(local_count, 128, pivots)
    update = child_update.reshape(local_count, 128, window_cols)
    entries = parent_entries.reshape(local_rows, 128 * half, 128)

    all_maps = child_map.reshape(pair_count, local_count, proc_count)
    child_maps = lax.dynamic_index_in_dim(all_maps, my_pair, 0, False)
    inside = child_maps < proc_count
    lead_at = jnp.argmax(inside.astype(jnp.int32), axis=0)
    all_ids = jnp.min(jnp.where(all_maps < proc_count, all_maps, proc_count), axis=1)
    all_seats = jnp.argmax(
        (all_ids[:, None, :] == jnp.arange(proc_count)[None, :, None]).astype(jnp.int32), axis=2
    ).astype(jnp.int32)
    seats = lax.dynamic_index_in_dim(all_seats, my_pair, 0, False)
    own_blocks = lax.dynamic_index_in_dim(child_maps, my_proc, 1, False)
    target = own_blocks % proc_count
    order = jnp.arange(local_count)
    rank = jnp.sum(
        ((target[:, None] == target[None, :]) & (order[None, :] < order[:, None])).astype(jnp.int32),
        axis=1,
    )
    slots = (target * capacity + rank).astype(jnp.int32)
    hit = all_maps % proc_count == my_proc
    hit_rank = jnp.cumsum(hit.astype(jnp.int32), axis=1) - 1
    source = (
        jnp.arange(pair_count)[:, None, None] * proc_count + jnp.arange(proc_count)[None, None, :]
    ) * capacity + hit_rank
    match = hit[..., None] & (all_maps[..., None] // proc_count == jnp.arange(local_rows))
    where = jnp.max(jnp.where(match, source[..., None], -1), axis=(1, 2))
    where = where.reshape(pair_count * local_rows).astype(jnp.int32)

    my_lead = lax.dynamic_index_in_dim(lead_at, my_proc, 0, False)
    picked = lax.dynamic_index_in_dim(factor, my_lead, 0, True)
    gathered = lax.all_gather(picked, "proc", axis=0, tiled=True)
    ends = jnp.concatenate(
        [lax.dynamic_index_in_dim(gathered, seats[k], 0, False) for k in range(PANELS)], axis=0
    )
    lead_part = lax.dynamic_slice(
        update, (my_lead, 0, 0), (1, 128, PANELS * 128)
    )[0] - lax.dot_general(picked[0], ends, NT, preferred_element_type=jnp.float32)
    lead_sent = jnp.concatenate([lead_part, entries[0, ::half]], axis=1)
    lead_all = lax.all_gather(lead_sent, ("pair", "proc"), axis=0, tiled=False)
    lead_all = lead_all.reshape(2, proc_count, 128, (PANELS + 1) * 128)
    packed = contrib_blocks(factor, update, gathered, slots, seats, slot_count, 4)
    arrived = lax.all_to_all(
        packed.astype(LINK).reshape(pair_count * proc_count, capacity, 128, half * 128),
        ("pair", "proc"),
        split_axis=0,
        concat_axis=0,
        tiled=True,
    ).reshape(pair_count * slot_count, 128, half * 128)
    arrived = arrived.astype(jnp.float32)

    shares = [
        jnp.stack(
            [lax.dynamic_index_in_dim(lead_all[c], all_seats[c, d], 0, False) for d in range(proc_count)]
        )
        for c in range(2)
    ]
    lead = jnp.stack(
        [
            lead_all[k, :, :, PANELS * 128 :]
            + (shares[0] + shares[1])[:, :, k * 128 : (k + 1) * 128]
            for k in range(PANELS)
        ]
    )
    column = raw_column(entries, arrived, where, 4)
    other = lax.ppermute(column.astype(LINK), "pair", [(0, 1), (1, 0)]).astype(jnp.float32)
    own_lead = lax.dynamic_index_in_dim(lead, my_proc, 1, False)
    first_row = (jnp.arange(local_rows) == 0)[:, None, None]
    zero = jnp.where(first_row, own_lead[0], jnp.where(my_pair == 0, column, other))
    one = jnp.where(first_row, own_lead[1], jnp.where(my_pair == 0, other, column))

    ids = jnp.arange(block_cols)[:, None, None]
    pivot0, inverse0 = pivot_of(lead[0, 0])
    first = jnp.where(ids > 0, times_t(lead[0, :block_cols], inverse0), pivot0)
    rest = lead[1, :block_cols] - times_t(first, first[1])
    pivot1, inverse1 = pivot_of(rest[1])
    second = jnp.where(ids > 1, times_t(rest, inverse1), jnp.where(ids == 1, pivot1, 0.0))
    both = jnp.concatenate([first, second], axis=2)
    mine = lax.dynamic_index_in_dim(both.reshape(half, 2, 128, 256), my_pair, 1, False)
    small = jnp.stack([inverse0, pivot0, inverse1, pivot1, first[1]])
    place = jnp.stack([my_proc, my_pair, jnp.int32(proc_count)]).astype(jnp.int32)
    result = finish(
        entries, arrived, where, place, zero, one, small, mine.reshape(half * 128, 256), 4
    )
    return result.reshape(local_rows, 1, 128, half, 1, 128)


def solution(mesh):
    in_specs = (
        P("pair", "grp", "proc", None, None),
        P("pair", "grp", "proc", None, None),
        P(None, "grp"),
        P("grp", "proc", None, None, "pair", None),
    )
    out_specs = P("grp", "proc", None, None, "pair", None)
    return jax.shard_map(body, mesh=mesh, in_specs=in_specs, out_specs=out_specs, check_vma=False)
```

```python
import functools

import jax
import jax.numpy as jnp
from jax import lax
from jax.experimental import pallas as pl
from jax.experimental.pallas import tpu as pltpu
from jax.sharding import PartitionSpec as P

HIGHEST = lax.Precision.HIGHEST
NT = (((1,), (1,)), ((), ()))
PANELS = 2
LINK = jnp.float16
VMEM_LIMIT = 60 * 1024 * 1024


def halves(x):
    high = x.astype(jnp.bfloat16)
    return high, (x - high.astype(jnp.float32)).astype(jnp.bfloat16)


def nt_dot(a, b):
    a_high, a_low = halves(a)
    b_high, b_low = halves(b)
    return lax.dot_general(
        jnp.concatenate([a_high, a_high, a_low], axis=1),
        jnp.concatenate([b_high, b_low, b_high], axis=1),
        NT,
        preferred_element_type=jnp.float32,
    )


def contrib_kernel(group, half, slots, seats, factor_ref, update_ref, *rest):
    window_refs, out_ref, window = rest[: 2 * half], rest[2 * half], rest[2 * half + 1]
    step = pl.program_id(0)

    @pl.when(step == 0)
    def _():
        for p in range(2):
            for h in range(half):
                window[p, h * 128 : (h + 1) * 128, :] = window_refs[2 * h + p][0]

    pivots = factor_ref.shape[2]
    rows = factor_ref[...].reshape(group * 128, pivots)
    for p in range(2):
        product = lax.dot_general(rows, window[p], NT, preferred_element_type=jnp.float32)
        for g in range(group):
            slot = slots[step * group + g]
            for h in range(half):
                w = 2 * h + p
                out_ref[p, slot, :, h * 128 : (h + 1) * 128] = (
                    update_ref[g, :, w * 128 : (w + 1) * 128]
                    - product[g * 128 : (g + 1) * 128, h * 128 : (h + 1) * 128]
                ).astype(out_ref.dtype)


def contrib_blocks(factor, update, gathered, slots, seats, slot_count, group):
    rows, _, pivots = factor.shape
    cols = update.shape[2]
    half = cols // 256
    once = pl.Buffered(1)

    def seat_map(w):
        return lambda i, slots, seats: (seats[w], 0, 0)

    return pl.pallas_call(
        functools.partial(contrib_kernel, group, half),
        out_shape=jax.ShapeDtypeStruct((2, slot_count, 128, half * 128), jnp.float32),
        grid_spec=pltpu.PrefetchScalarGridSpec(
            num_scalar_prefetch=2,
            grid=(rows // group,),
            in_specs=[
                pl.BlockSpec((group, 128, pivots), lambda i, slots, seats: (i, 0, 0)),
                pl.BlockSpec((group, 128, cols), lambda i, slots, seats: (i, 0, 0)),
            ]
            + [
                pl.BlockSpec((1, 128, pivots), seat_map(w), pipeline_mode=once)
                for w in range(2 * half)
            ],
            out_specs=pl.BlockSpec(
                (2, slot_count, 128, half * 128),
                lambda i, slots, seats: (0, 0, 0, 0),
                pipeline_mode=once,
            ),
            scratch_shapes=[pltpu.VMEM((2, half * 128, pivots), jnp.bfloat16)],
        ),
        cost_estimate=pl.CostEstimate(
            flops=2 * rows * 128 * cols * pivots,
            bytes_accessed=rows * 128 * (2 * pivots + 6 * cols) + 2 * cols * pivots,
            transcendentals=0,
        ),
        compiler_params=pltpu.CompilerParams(vmem_limit_bytes=VMEM_LIMIT),
        name="contrib",
    )(slots, seats, factor, update, *([gathered] * (2 * half)))


def column_kernel(group, half, where, entries_ref, *rest):
    arrived, out_ref = rest[: 2 * group], rest[2 * group]
    step = pl.program_id(0)
    count = where.shape[0] // 2
    for g in range(group):
        value = entries_ref[g, pl.ds(0, 128, stride=half), :]
        for c in range(2):
            spot = where[c * count + step * group + g]
            part = arrived[2 * g + c][0].astype(jnp.float32)
            value = value + jnp.where(spot >= 0, part, 0.0)
        out_ref[g] = value


def arrived_specs(group, count, width):
    def spot(c, g):
        return lambda i, where, *more: (jnp.maximum(where[c * count + i * group + g], 0), 0, 0)

    return [pl.BlockSpec((1, 128, width), spot(c, g)) for g in range(group) for c in range(2)]


def raw_column(entries, arrived, where, group):
    count, rows, _ = entries.shape
    half = rows // 128
    return pl.pallas_call(
        functools.partial(column_kernel, group, half),
        out_shape=jax.ShapeDtypeStruct((count, 128, 128), jnp.float32),
        grid_spec=pltpu.PrefetchScalarGridSpec(
            num_scalar_prefetch=1,
            grid=(count // group,),
            in_specs=[pl.BlockSpec((group, rows, 128), lambda i, where: (i, 0, 0))]
            + arrived_specs(group, count, 128),
            out_specs=pl.BlockSpec((group, 128, 128), lambda i, where: (i, 0, 0)),
        ),
        compiler_params=pltpu.CompilerParams(vmem_limit_bytes=VMEM_LIMIT),
        name="raw_column",
    )(where, entries, *([arrived] * (2 * group)))


def finish_kernel(group, half, where, place, entries_ref, zero_ref, one_ref, small_ref, lead_ref, *rest):
    arrived, out_ref = rest[: 2 * group], rest[2 * group]
    step = pl.program_id(0)
    count = where.shape[0] // 2
    my_proc, my_pair, proc_count = place[0], place[1], place[2]
    rows = group * 128
    block = (step * group + lax.broadcasted_iota(jnp.int32, (rows, 1), 0) // 128) * proc_count + my_proc

    def spread(k):
        return jnp.broadcast_to(small_ref[k][None], (group, 128, 128)).reshape(rows, 128)

    first = nt_dot(zero_ref[...].reshape(rows, 128), small_ref[0])
    first = jnp.where(block > 0, first, spread(1))
    second = nt_dot(one_ref[...].reshape(rows, 128) - nt_dot(first, small_ref[4]), small_ref[2])
    second = jnp.where(block > 1, second, jnp.where(block == 1, spread(3), 0.0))
    change = nt_dot(jnp.concatenate([first, second], axis=1), lead_ref[128:, :])
    row_id = block * 128 + lax.broadcasted_iota(jnp.int32, (rows, 1), 0) % 128
    lane = lax.broadcasted_iota(jnp.int32, (1, 128), 1)
    panel = jnp.where(my_pair == 0, first, second)
    for h in range(half):
        lower = row_id >= (2 * h + my_pair) * 128 + lane
        for g in range(group):
            span = slice(g * 128, (g + 1) * 128)
            if h == 0:
                value = panel[span]
            else:
                value = entries_ref[g, pl.ds(h, 128, stride=half), :]
                for c in range(2):
                    spot = where[c * count + step * group + g]
                    part = arrived[2 * g + c][0, :, h * 128 : (h + 1) * 128].astype(jnp.float32)
                    value = value + jnp.where(spot >= 0, part, 0.0)
                value = value - change[span, (h - 1) * 128 : h * 128]
            out_ref[g, pl.ds(h, 128, stride=half), :] = jnp.where(lower[span], value, 0.0)


def finish(entries, arrived, where, place, zero, one, small, lead, group):
    count, rows, _ = entries.shape
    half = rows // 128
    by_row = lambda i, where, place: (i, 0, 0)
    return pl.pallas_call(
        functools.partial(finish_kernel, group, half),
        out_shape=jax.ShapeDtypeStruct(entries.shape, jnp.float32),
        grid_spec=pltpu.PrefetchScalarGridSpec(
            num_scalar_prefetch=2,
            grid=(count // group,),
            in_specs=[
                pl.BlockSpec((group, rows, 128), by_row),
                pl.BlockSpec((group, 128, 128), by_row),
                pl.BlockSpec((group, 128, 128), by_row),
                pl.BlockSpec(small.shape, lambda i, where, place: (0, 0, 0)),
                pl.BlockSpec(lead.shape, lambda i, where, place: (0, 0)),
            ]
            + arrived_specs(group, count, half * 128),
            out_specs=pl.BlockSpec((group, rows, 128), by_row),
        ),
        compiler_params=pltpu.CompilerParams(vmem_limit_bytes=VMEM_LIMIT),
        name="finish",
    )(where, place, entries, zero, one, small, lead, *([arrived] * (2 * group)))


def pivot_of(block):
    pivot = jnp.linalg.cholesky(jnp.tril(block) + jnp.tril(block, -1).T)
    inverse = lax.linalg.triangular_solve(
        pivot, jnp.eye(128, dtype=jnp.float32), left_side=True, lower=True
    )
    return pivot, inverse


def times_t(a, b):
    return jnp.einsum("qax,bx->qab", a, b, precision=HIGHEST)


def body(child_factor, child_update, child_map, parent_entries):
    proc_count = lax.axis_size("proc")
    pair_count = lax.axis_size("pair")
    my_proc = lax.axis_index("proc")
    my_pair = lax.axis_index("pair")
    _, local_count, _, _, pivots = child_factor.shape
    window_cols = child_update.shape[4]
    block_cols = window_cols // 128
    half = block_cols // 2
    capacity = -(-local_count // proc_count)
    slot_count = proc_count * capacity
    local_rows = parent_entries.shape[0]
    factor = child_factor.reshape(local_count, 128, pivots)
    update = child_update.reshape(local_count, 128, window_cols)
    entries = parent_entries.reshape(local_rows, 128 * half, 128)

    all_maps = child_map.reshape(pair_count, local_count, proc_count)
    child_maps = lax.dynamic_index_in_dim(all_maps, my_pair, 0, False)
    inside = child_maps < proc_count
    lead_at = jnp.argmax(inside.astype(jnp.int32), axis=0)
    all_ids = jnp.min(jnp.where(all_maps < proc_count, all_maps, proc_count), axis=1)
    all_seats = jnp.argmax(
        (all_ids[:, None, :] == jnp.arange(proc_count)[None, :, None]).astype(jnp.int32), axis=2
    ).astype(jnp.int32)
    seats = lax.dynamic_index_in_dim(all_seats, my_pair, 0, False)
    own_blocks = lax.dynamic_index_in_dim(child_maps, my_proc, 1, False)
    target = own_blocks % proc_count
    order = jnp.arange(local_count)
    rank = jnp.sum(
        ((target[:, None] == target[None, :]) & (order[None, :] < order[:, None])).astype(jnp.int32),
        axis=1,
    )
    slots = (target * capacity + rank).astype(jnp.int32)
    hit = all_maps % proc_count == my_proc
    hit_rank = jnp.cumsum(hit.astype(jnp.int32), axis=1) - 1
    source = (
        jnp.arange(pair_count)[:, None, None] * proc_count + jnp.arange(proc_count)[None, None, :]
    ) * capacity + hit_rank
    match = hit[..., None] & (all_maps[..., None] // proc_count == jnp.arange(local_rows))
    where = jnp.max(jnp.where(match, source[..., None], -1), axis=(1, 2))
    where = where.reshape(pair_count * local_rows).astype(jnp.int32)

    my_lead = lax.dynamic_index_in_dim(lead_at, my_proc, 0, False)
    picked = lax.dynamic_index_in_dim(factor, my_lead, 0, True)
    gathered = lax.all_gather(picked, "proc", axis=0, tiled=True)
    ends = jnp.concatenate(
        [lax.dynamic_index_in_dim(gathered, seats[k], 0, False) for k in range(PANELS)], axis=0
    )
    lead_part = lax.dynamic_slice(
        update, (my_lead, 0, 0), (1, 128, PANELS * 128)
    )[0] - lax.dot_general(picked[0], ends, NT, preferred_element_type=jnp.float32)
    lead_sent = jnp.concatenate([lead_part, entries[0, ::half]], axis=1)
    lead_all = lax.all_gather(lead_sent, ("pair", "proc"), axis=0, tiled=False)
    lead_all = lead_all.reshape(2, proc_count, 128, (PANELS + 1) * 128)
    packed = contrib_blocks(factor, update, gathered, slots, seats, slot_count, 4)
    arrived = lax.all_to_all(
        packed.astype(LINK).reshape(pair_count * proc_count, capacity, 128, half * 128),
        ("pair", "proc"),
        split_axis=0,
        concat_axis=0,
        tiled=True,
    ).reshape(pair_count * slot_count, 128, half * 128)
    arrived = arrived.astype(jnp.float32)

    shares = [
        jnp.stack(
            [lax.dynamic_index_in_dim(lead_all[c], all_seats[c, d], 0, False) for d in range(proc_count)]
        )
        for c in range(2)
    ]
    lead = jnp.stack(
        [
            lead_all[k, :, :, PANELS * 128 :]
            + (shares[0] + shares[1])[:, :, k * 128 : (k + 1) * 128]
            for k in range(PANELS)
        ]
    )
    column = raw_column(entries, arrived, where, 6)
    other = lax.ppermute(column.astype(LINK), "pair", [(0, 1), (1, 0)]).astype(jnp.float32)
    own_lead = lax.dynamic_index_in_dim(lead, my_proc, 1, False)
    first_row = (jnp.arange(local_rows) == 0)[:, None, None]
    zero = jnp.where(first_row, own_lead[0], jnp.where(my_pair == 0, column, other))
    one = jnp.where(first_row, own_lead[1], jnp.where(my_pair == 0, other, column))

    ids = jnp.arange(block_cols)[:, None, None]
    pivot0, inverse0 = pivot_of(lead[0, 0])
    first = jnp.where(ids > 0, times_t(lead[0, :block_cols], inverse0), pivot0)
    rest = lead[1, :block_cols] - times_t(first, first[1])
    pivot1, inverse1 = pivot_of(rest[1])
    second = jnp.where(ids > 1, times_t(rest, inverse1), jnp.where(ids == 1, pivot1, 0.0))
    both = jnp.concatenate([first, second], axis=2)
    mine = lax.dynamic_index_in_dim(both.reshape(half, 2, 128, 256), my_pair, 1, False)
    small = jnp.stack([inverse0, pivot0, inverse1, pivot1, first[1]])
    place = jnp.stack([my_proc, my_pair, jnp.int32(proc_count)]).astype(jnp.int32)
    result = finish(
        entries, arrived, where, place, zero, one, small, mine.reshape(half * 128, 256), 4
    )
    return result.reshape(local_rows, 1, 128, half, 1, 128)


def solution(mesh):
    in_specs = (
        P("pair", "grp", "proc", None, None),
        P("pair", "grp", "proc", None, None),
        P(None, "grp"),
        P("grp", "proc", None, None, "pair", None),
    )
    out_specs = P("grp", "proc", None, None, "pair", None)
    return jax.shard_map(body, mesh=mesh, in_specs=in_specs, out_specs=out_specs, check_vma=False)
```
